32 devices in a mesh: dp: 4 (over z), expert: 8 (over y, x, core).
Axes of the slice: x: 2, y: 2, z: 4, core: 2. Of those that a mesh axis runs over, the one named last changes fastest.
Arguments:
- first_out: bfloat16 [4096, 1024], P(('dp', 'expert')), may hold values from -6 to 6
- second_out: bfloat16 [4096, 1024], P(('dp', 'expert')), may hold values from -6 to 6
- first_grad: bfloat16 [4096, 1024], P(('dp', 'expert')), may hold values from -6 to 6
- second_grad: bfloat16 [4096, 1024], P(('dp', 'expert')), may hold values from -6 to 6
- routes: int32 [4096, 2], P(('dp', 'expert')), may hold values from 0 to 7, all different within a row; in each aligned block of 128 rows (0 to 127, 128 to 255, ...) at most 64 rows name the same one
- gate_values: float32 [4096, 2], P(('dp', 'expert')), may hold values from 0.1 to 1
- w_gate: bfloat16 [8, 1024, 768], P('expert', 'dp'), may hold values from -0.1875 to 0.1875
- w_up: bfloat16 [8, 1024, 768], P('expert', 'dp'), may hold values from -0.1875 to 0.1875
- w_down: bfloat16 [8, 1024, 768], P('expert', 'dp'), may hold values from -0.21875 to 0.21875
Outputs:
- second_in: bfloat16 [4096, 1024], P(('dp', 'expert'))
- first_total: bfloat16 [4096, 1024], P(('dp', 'expert'))
- gate_grad: float32 [4096, 2], P(('dp', 'expert'))
- w_down_grad: float32 [8, 1024, 768], P('expert', 'dp')
The draws below stay inside these ranges and needn't reach their ends.
Inputs may be any that keep to these rules, and one draw needn't show every extreme that they name: `routes`: each row names 2 different experts. Among the 128 rows of one device no expert is named more than 64 times, and in every draw some device names some expert exactly 64 times.
All inputs are finite; a program needn't handle non-finite values.
Results may differ from the reference program's by a relative error of at most 0.0051.
Values may be sent and summed in bfloat16 or wider, within the bound.
A program may use at most 64 MiB of HBM per device.

```python
import math
import jax
import jax.numpy as jnp
import numpy as np
from jax import lax

D = 1024
H = 768
TOP = 2
TOK_DEV = 128
EXPERTS = 8
CAP = 64
ROWS_COL = 512
TOKENS = 4096


def level_of(rng, extent, pieces, smallest, largest):
    gain = 1.0
    for axis_at, blocks in pieces:
        draws = jax.random.uniform(jax.random.fold_in(jax.random.fold_in(rng, 6), axis_at), (blocks,), jnp.float32, smallest / len(pieces), largest / len(pieces))
        gain = gain * jnp.repeat(jnp.exp(draws), extent[axis_at] // blocks).reshape((-1,) + (1,) * (len(extent) - 1 - axis_at))
    return gain


def deal_out(rng, own, number, rows, count, top, reach, lean):
    sequence = jax.random.permutation(rng, count)
    heavy_load, usual = portions_of(count, rows * top, reach, lean, True), portions_of(count, rows * top, reach, lean, False)
    places = jnp.arange(count)

    def named(lengths, rotation):
        used = int((lengths > 0).sum())
        fixed = max(1, used // 4)
        moved = fixed + (places - fixed + rotation * (used - fixed)) % max(1, count - fixed)
        return jnp.zeros((count,), jnp.int32).at[sequence[jnp.where(places < fixed, places, moved)]].set(jnp.asarray(lengths, jnp.int32))

    lengths = jnp.where(number % 4 == 0, named(heavy_load, number // 4), named(usual, number - number // 4 - 1))
    mixed = jax.random.permutation(jax.random.fold_in(own, 3), count)
    donor, receiver = mixed[0:count // 2 * 2:2], mixed[1:count // 2 * 2:2]
    room = jnp.minimum(lengths[donor] - 1, reach - lengths[receiver]) // 2
    room = jnp.where((donor == sequence[0]) | (receiver == sequence[0]) | (lengths[receiver] == 0), 0, jnp.maximum(room, 0))
    moved = jax.random.randint(jax.random.fold_in(own, 4), (count // 2,), 0, 1 << 20) % (room + 1)
    lengths = lengths.at[donor].add(-moved).at[receiver].add(moved)
    members = jnp.searchsorted(jnp.cumsum(lengths), jnp.arange(rows * top), side="right").astype(jnp.int32)
    table = members.reshape(top, rows).T
    table = table[jax.random.permutation(jax.random.fold_in(own, 1), rows)]
    rotation = jax.random.randint(jax.random.fold_in(own, 2), (rows, 1), 0, top)
    return jnp.take_along_axis(table, (jnp.arange(top)[None, :] + rotation) % top, axis=1)


def portions_of(number_of, total, reach, slope, full):
    portions = [(1 << 20) // math.isqrt(grade ** slope) + 1 for grade in range(1, number_of + 1)]
    largest = reach if full else min(reach, max(-(-total // number_of), total * portions[0] // sum(portions)))
    least = 1 if total - largest >= number_of - 1 else 0
    given, spare = [largest] + [least] * (number_of - 1), total - largest - least * (number_of - 1)
    while spare > 0:
        movable = [i for i in range(1, number_of) if given[i] < largest] or [i for i in range(1, number_of) if given[i] < reach]
        mass, budget = sum([portions[i] for i in movable]), spare
        for i in movable:
            addition = min(reach - given[i], max(1, budget * portions[i] // mass), spare)
            given[i] = given[i] + addition
            spare = spare - addition
    return np.array(given)


def bell_draw(stream_key, shape, spread, bound, cuts=(), kind=jnp.bfloat16):
    level = level_of(stream_key, shape, cuts, -0.22, 0.18) if cuts else 1.0
    values = jax.random.normal(stream_key, shape, jnp.float32) * spread * level
    return jnp.minimum(jnp.maximum(values, -bound), bound).astype(kind)


def setup_inputs(seed: int = 0) -> dict:
    splits = jax.random.split(jax.random.key(seed), 10)
    first_out = bell_draw(splits[0], (TOKENS, D), 1.0, 6.0, ((0, 32),))
    second_out = bell_draw(splits[1], (TOKENS, D), 1.0, 6.0, ((0, 32),))
    first_grad = bell_draw(splits[2], (TOKENS, D), 1.0, 6.0, ((0, 32),))
    second_grad = bell_draw(splits[3], (TOKENS, D), 1.0, 6.0, ((0, 32),))
    routes_keys = jax.random.split(jax.random.fold_in(splits[4], 1), TOKENS // TOK_DEV)
    routes_turns = jax.random.permutation(jax.random.fold_in(splits[4], 3), TOKENS // TOK_DEV)
    routes = jax.vmap(lambda own, number: deal_out(jax.random.fold_in(splits[4], 2), own, number, TOK_DEV, EXPERTS, TOP, CAP, 2))(routes_keys, routes_turns).reshape((TOKENS, TOP))
    gate_values = jnp.clip(0.1 + 0.9 * jax.random.uniform(splits[5], (TOKENS, TOP), jnp.float32) ** level_of(splits[5], (TOKENS, TOP), ((0, 32),), -0.2, 0.2), 0.1, 1.0)
    w_gate = bell_draw(splits[6], (EXPERTS, D, H), D ** -0.5, 0.1875, ((0, 8), (1, 4)))
    w_up = bell_draw(splits[7], (EXPERTS, D, H), D ** -0.5, 0.1875, ((0, 8), (1, 4)))
    w_down = bell_draw(splits[8], (EXPERTS, D, H), H ** -0.5, 0.21875, ((0, 8), (1, 4)))
    return dict(first_out=first_out, second_out=second_out, first_grad=first_grad, second_grad=second_grad, routes=routes, gate_values=gate_values, w_gate=w_gate, w_up=w_up, w_down=w_down)


def expert_rows(rows_in, rows_cot, gate_mat, up_mat, down_mat):
    pre_gate = jnp.dot(rows_in, gate_mat, preferred_element_type=jnp.float32)
    pre_up = jnp.dot(rows_in, up_mat, preferred_element_type=jnp.float32)
    squashed = jax.nn.sigmoid(pre_gate)
    activated = pre_gate * squashed
    hidden = (activated * pre_up).astype(jnp.bfloat16)
    out_rows = lax.dot_general(hidden, down_mat, (((1,), (1,)), ((), ())), preferred_element_type=jnp.float32).astype(jnp.bfloat16)
    hidden_cot = jnp.dot(rows_cot, down_mat, preferred_element_type=jnp.float32)
    gate_cot = (hidden_cot * pre_up * squashed * (1.0 + pre_gate * (1.0 - squashed))).astype(jnp.bfloat16)
    up_cot = (hidden_cot * activated).astype(jnp.bfloat16)
    input_cot = lax.dot_general(gate_cot, gate_mat, (((1,), (1,)), ((), ())), preferred_element_type=jnp.float32)
    input_cot = input_cot + lax.dot_general(up_cot, up_mat, (((1,), (1,)), ((), ())), preferred_element_type=jnp.float32)
    return (out_rows, input_cot.astype(jnp.bfloat16), hidden)

def reference(first_out, second_out, first_grad, second_grad, routes, gate_values, w_gate, w_up, w_down):
    assigned = TOKENS * TOP
    expert_ids = routes.reshape(assigned).astype(jnp.int32)
    token_of = jnp.arange(assigned, dtype=jnp.int32) // TOP
    out_cot_all = (gate_values.reshape(assigned)[:, None] * second_grad[token_of].astype(jnp.float32)).astype(jnp.bfloat16)
    sort_order = jnp.argsort(expert_ids, stable=True).astype(jnp.int32)
    counts = lax.optimization_barrier(jnp.sum((expert_ids[:, None] == jnp.arange(EXPERTS, dtype=jnp.int32)[None, :]).astype(jnp.int32), axis=0))
    starts = (jnp.cumsum(counts) - counts).astype(jnp.int32)
    block_rows = 1024
    order_pad = jnp.concatenate([sort_order, jnp.full((block_rows,), assigned, jnp.int32)])

    def per_expert(scan_carry, inputs):
        first_start, row_count, gate_mat, up_mat, down_mat = inputs

        def per_block(block_step, loop_state):
            out_acc, cot_acc, grad_acc = loop_state
            offset = (block_step * block_rows).astype(jnp.int32)
            row_index = lax.dynamic_slice_in_dim(order_pad, (first_start + offset).astype(jnp.int32), block_rows)
            in_range = offset + jnp.arange(block_rows, dtype=jnp.int32) < row_count
            row_index = jnp.where(in_range, row_index, assigned).astype(jnp.int32)
            safe_index = jnp.minimum(row_index, assigned - 1)
            rows_in = jnp.where(in_range[:, None], first_out[safe_index // TOP], jnp.zeros((), jnp.bfloat16))
            rows_cot = jnp.where(in_range[:, None], out_cot_all[safe_index], jnp.zeros((), jnp.bfloat16))
            out_rows, input_cot, hidden = expert_rows(rows_in, rows_cot, gate_mat, up_mat, down_mat)
            grad_acc = grad_acc + lax.dot_general(rows_cot, hidden, (((0,), (0,)), ((), ())), preferred_element_type=jnp.float32)
            out_acc = out_acc.at[row_index].set(out_rows, mode='drop')
            cot_acc = cot_acc.at[row_index].set(input_cot, mode='drop')
            return (out_acc, cot_acc, grad_acc)
        blocks = (row_count + block_rows - 1) // block_rows
        out_acc, cot_acc, grad_acc = lax.fori_loop(0, blocks, per_block, (scan_carry[0], scan_carry[1], jnp.zeros((D, H), jnp.float32)))
        return ((out_acc, cot_acc), grad_acc)
    empty_rows = jnp.zeros((assigned, D), jnp.bfloat16)
    (out_acc, cot_acc), grad_stack = lax.scan(per_expert, (empty_rows, empty_rows), (starts, counts, w_gate, w_up, w_down))
    expert_out = out_acc.reshape(TOKENS, TOP, D).astype(jnp.float32)
    combined = lax.optimization_barrier(jnp.sum(gate_values[:, :, None] * expert_out, axis=1))
    second_in = (second_out.astype(jnp.float32) - combined).astype(jnp.bfloat16)
    gate_grad = lax.optimization_barrier(jnp.sum(second_grad.astype(jnp.float32)[:, None, :] * expert_out, axis=2))
    first_total = (first_grad.astype(jnp.float32) + lax.optimization_barrier(jnp.sum(cot_acc.reshape(TOKENS, TOP, D).astype(jnp.float32), axis=1))).astype(jnp.bfloat16)
    w_down_grad = grad_stack * (1.0 / math.sqrt(ROWS_COL))
    return (second_in, first_total, gate_grad, w_down_grad)
```

```python
import functools
import math

import jax
import jax.numpy as jnp
from jax import lax
from jax.experimental import pallas as pl
from jax.experimental.pallas import tpu as pltpu
from jax.sharding import PartitionSpec as P

BF = jnp.bfloat16
F32 = jnp.float32
MESH = pl.DeviceIdType.MESH


def mm(a, b, ca, cb):
    return lax.dot_general(a, b, (((ca,), (cb,)), ((), ())), preferred_element_type=F32)


def tiles(extent, size=256):
    size = min(size, extent)
    return [slice(at, at + size) for at in range(0, extent, size)]


def layer_kernel(
    n, owners, cap, scale,
    x_ref, so_ref, fg_ref, sg_ref, routes_ref, gv_ref, wg_hbm, wu_hbm, wd_hbm,
    si_ref, ft_ref, gg_ref, wdg_ref,
    wbuf, s_in, s_cot, r_in, r_cot, hid, act, fac, gc, uc,
    o_out, b_out, o_cot, b_cot, part, rs_send, rs_recv, qbuf,
    lsem, wss, wrs, ass, ars, oss, ors, css, crs, rss, rrs,
):
    z = lax.axis_index("dp")
    me = lax.axis_index("expert")
    count, width = x_ref.shape
    top = routes_ref.shape[1]
    slots = owners * cap
    depth, units = wbuf.shape[2], wbuf.shape[3]

    def peers(body):
        def step(o, carry):
            body(o, lax.rem(me + o, owners))
            return carry
        lax.fori_loop(1, owners, step, 0)

    barrier = pltpu.get_barrier_semaphore()
    peers(lambda o, to: pl.semaphore_signal(
        barrier, inc=1, device_id={"expert": to}, device_id_type=MESH))

    @pl.when(z > 0)
    def _():
        pl.semaphore_signal(barrier, inc=1, device_id={"dp": z - 1}, device_id_type=MESH)

    @pl.when(z < n - 1)
    def _():
        pl.semaphore_signal(barrier, inc=1, device_id={"dp": z + 1}, device_id_type=MESH)

    local = [
        pltpu.make_async_copy(w.at[0], wbuf.at[m, z], lsem.at[m])
        for m, w in enumerate((wg_hbm, wu_hbm, wd_hbm))
    ]
    for copy in local:
        copy.start()

    routes = routes_ref[...]
    gates = gv_ref[...]
    ids = lax.broadcasted_iota(jnp.int32, (count, owners), 1)
    lower = (
        lax.broadcasted_iota(jnp.int32, (count, count), 1)
        < lax.broadcasted_iota(jnp.int32, (count, count), 0)
    ).astype(F32).astype(BF)
    slot_ids = lax.broadcasted_iota(jnp.int32, (count, slots), 1)
    base = jnp.zeros((1, owners), F32)
    for k in range(top):
        onehot = (routes[:, k:k + 1] == ids).astype(F32)
        before = mm(lower, onehot.astype(BF), 1, 0) + base
        place = jnp.sum(onehot * (before + ids.astype(F32) * cap), axis=1, keepdims=True)
        base = base + jnp.sum(onehot, axis=0, keepdims=True)
        qbuf[k] = (place.astype(jnp.int32) == slot_ids).astype(F32).astype(BF)

    def wcopy(m, s, way, shard, to):
        return pltpu.make_async_remote_copy(
            src_ref=wbuf.at[m, shard], dst_ref=wbuf.at[m, shard],
            send_sem=wss.at[way, m, s], recv_sem=wrs.at[way, m, s],
            device_id={"dp": to}, device_id_type=MESH)

    def wsend(m, s, finish=False):
        @pl.when((z >= s) & (z < n - 1))
        def _():
            copy = wcopy(m, s, 0, z - s, z + 1)
            copy.wait_send() if finish else copy.start()

        @pl.when((z + s <= n - 1) & (z > 0))
        def _():
            copy = wcopy(m, s, 1, z + s, z - 1)
            copy.wait_send() if finish else copy.start()

    def wrecv(m, s):
        @pl.when(z - 1 - s >= 0)
        def _():
            wcopy(m, s, 0, z - 1 - s, z - 1).wait_recv()

        @pl.when(z + 1 + s <= n - 1)
        def _():
            wcopy(m, s, 1, z + 1 + s, z + 1).wait_recv()

    for copy in local:
        copy.wait()
    pl.semaphore_wait(barrier, owners - 1 + jnp.minimum(z, 1) + jnp.minimum(n - 1 - z, 1))

    wsend(0, 0)
    wsend(1, 0)

    def acopy(a, o, to):
        src, dst = ((s_in, r_in), (s_cot, r_cot))[a]
        return pltpu.make_async_remote_copy(
            src_ref=src.at[to], dst_ref=dst.at[me],
            send_sem=ass.at[a, o], recv_sem=ars.at[a, o],
            device_id={"expert": to}, device_id_type=MESH)

    both = sum(qbuf[k].astype(F32) for k in range(top)).astype(BF)
    for c in tiles(width):
        rows = mm(both, x_ref[:, c], 0, 0).astype(BF)
        s_in[:, :, c] = rows.reshape(owners, cap, rows.shape[1])
    peers(lambda o, to: acopy(0, o, to).start())
    r_in[me] = s_in[me]
    for c in tiles(width):
        grads = sg_ref[:, c].astype(F32)
        rows = sum(
            mm(qbuf[k], (gates[:, k:k + 1] * grads).astype(BF), 0, 0) for k in range(top)
        ).astype(BF)
        s_cot[:, :, c] = rows.reshape(owners, cap, rows.shape[1])
    peers(lambda o, to: acopy(1, o, to).start())
    r_cot[me] = s_cot[me]

    for s in range(n - 1):
        for m in (0, 1):
            wrecv(m, s)
            if s + 1 < n - 1:
                wsend(m, s + 1)
        if s == max(n - 3, 0):
            wsend(2, 0)
    peers(lambda o, to: acopy(0, o, to).wait_recv())
    peers(lambda o, to: acopy(1, o, to).wait_recv())

    rows_in = r_in[...].reshape(slots, width)
    for c in tiles(units):
        size = c.stop - c.start
        pre_gate = mm(rows_in, wbuf[0, :, :, c].reshape(width, size), 1, 0)
        pre_up = mm(rows_in, wbuf[1, :, :, c].reshape(width, size), 1, 0)
        squashed = jax.nn.sigmoid(pre_gate)
        activated = pre_gate * squashed
        hid[:, c] = (activated * pre_up).astype(BF)
        act[:, c] = activated
        fac[:, c] = pre_up * squashed * (1.0 + pre_gate * (1.0 - squashed))

    def ocopy(j, o, to):
        return pltpu.make_async_remote_copy(
            src_ref=o_out.at[j, to], dst_ref=b_out.at[j, me],
            send_sem=oss.at[j, o], recv_sem=ors.at[j, o],
            device_id={"expert": to}, device_id_type=MESH)

    def out_shard(j):
        rows = mm(hid[...], wbuf[2, j], 1, 1).astype(BF)
        o_out[j] = rows.reshape(owners, cap, depth)
        peers(lambda o, to: ocopy(j, o, to).start())
        b_out[j, me] = o_out[j, me]

    out_shard(z)

    for c in tiles(width):
        part[c, :] = mm(r_cot[:, :, c].reshape(slots, c.stop - c.start), hid[...], 0, 0)

    def rcopy(way, j, to):
        return pltpu.make_async_remote_copy(
            src_ref=rs_send.at[j], dst_ref=rs_recv.at[way, j],
            send_sem=rss.at[way, j], recv_sem=rrs.at[way, j],
            device_id={"dp": to}, device_id_type=MESH)

    def rstep(way, j):
        behind = z - 1 if way == 0 else z + 1
        ahead = z + 1 if way == 0 else z - 1
        first = z == 0 if way == 0 else z == n - 1
        mine = part[j * depth:(j + 1) * depth, :]

        @pl.when(z < j if way == 0 else z > j)
        def _():
            @pl.when(first)
            def _():
                rs_send[j] = mine.astype(BF)

            @pl.when(jnp.logical_not(first))
            def _():
                rcopy(way, j, behind).wait_recv()
                rs_send[j] = (mine + rs_recv[way, j].astype(F32)).astype(BF)

            rcopy(way, j, ahead).start()

    for s in range(n - 1):
        wrecv(2, s)
        if s + 1 < n - 1:
            wsend(2, s + 1)
        rstep(0, n - 1 - s)
        rstep(1, s)

        @pl.when(z - 1 - s >= 0)
        def _():
            out_shard(z - 1 - s)

        @pl.when(z + 1 + s <= n - 1)
        def _():
            out_shard(z + 1 + s)

    rows_cot = r_cot[...].reshape(slots, width)
    for c in tiles(units):
        hidden_cot = mm(rows_cot, wbuf[2, :, :, c].reshape(width, c.stop - c.start), 1, 0)
        gc[:, c] = (hidden_cot * fac[:, c]).astype(BF)
        uc[:, c] = (hidden_cot * act[:, c]).astype(BF)

    def ccopy(j, o, to):
        return pltpu.make_async_remote_copy(
            src_ref=o_cot.at[j, to], dst_ref=b_cot.at[j, me],
            send_sem=css.at[j, o], recv_sem=crs.at[j, o],
            device_id={"expert": to}, device_id_type=MESH)

    def cot_shard(j, carry):
        rows = mm(gc[...], wbuf[0, j], 1, 1) + mm(uc[...], wbuf[1, j], 1, 1)
        o_cot[j] = rows.astype(BF).reshape(owners, cap, depth)
        peers(lambda o, to: ccopy(j, o, to).start())
        b_cot[j, me] = o_cot[j, me]
        return carry

    lax.fori_loop(0, n, cot_shard, 0)

    sums = [jnp.zeros((count, 1), F32) for _ in range(top)]
    for j in range(n):
        c = slice(j * depth, (j + 1) * depth)
        peers(lambda o, to: ocopy(j, o, to).wait_recv())
        rows = b_out[j].reshape(slots, depth)
        combined = jnp.zeros((count, depth), F32)
        grads = sg_ref[:, c].astype(F32)
        for k in range(top):
            chosen = mm(qbuf[k], rows, 1, 0)
            combined = combined + gates[:, k:k + 1] * chosen
            sums[k] = sums[k] + jnp.sum(grads * chosen, axis=1, keepdims=True)
        si_ref[:, c] = (so_ref[:, c].astype(F32) - combined).astype(BF)
    for k in range(top):
        gg_ref[:, k:k + 1] = sums[k]

    own = pl.ds(pl.multiple_of(z * depth, depth), depth)

    @pl.when(z > 0)
    def _():
        rcopy(0, z, z - 1).wait_recv()
        part[own, :] = part[own, :] + rs_recv[0, z].astype(F32)

    @pl.when(z < n - 1)
    def _():
        rcopy(1, z, z + 1).wait_recv()
        part[own, :] = part[own, :] + rs_recv[1, z].astype(F32)

    wdg_ref[0] = part[own, :] * scale

    both = sum(qbuf[k].astype(F32) for k in range(top)).astype(BF)
    for j in range(n):
        c = slice(j * depth, (j + 1) * depth)
        peers(lambda o, to: ccopy(j, o, to).wait_recv())
        total = mm(both, b_cot[j].reshape(slots, depth), 1, 0)
        ft_ref[:, c] = (fg_ref[:, c].astype(F32) + total).astype(BF)

    for s in range(n - 1):
        for m in (0, 1, 2):
            wsend(m, s, finish=True)

        @pl.when(z < n - 1 - s)
        def _():
            rcopy(0, n - 1 - s, z + 1).wait_send()

        @pl.when(z > s)
        def _():
            rcopy(1, s, z - 1).wait_send()

    for a in (0, 1):
        peers(lambda o, to: acopy(a, o, to).wait_send())

    def sent(j, carry):
        peers(lambda o, to: ocopy(j, o, to).wait_send())
        peers(lambda o, to: ccopy(j, o, to).wait_send())
        return carry

    lax.fori_loop(0, n, sent, 0)


def per_device(
    first_out, second_out, first_grad, second_grad, routes, gate_values, w_gate, w_up, w_down
):
    count, width = first_out.shape
    top = routes.shape[1]
    owners = lax.axis_size("expert")
    n = lax.axis_size("dp")
    cap = min(count, 2 * count * top // owners)
    slots = owners * cap
    depth, units = w_gate.shape[1:]
    vmem = pl.BlockSpec(memory_space=pltpu.VMEM)
    hbm = pl.BlockSpec(memory_space=pl.ANY)
    dma = pltpu.SemaphoreType.DMA
    rows = pltpu.VMEM((owners, cap, width), BF)
    shards = pltpu.VMEM((n, owners, cap, depth), BF)
    return pl.pallas_call(
        functools.partial(layer_kernel, n, owners, cap, 1.0 / math.sqrt(count * n)),
        out_shape=(
            jax.ShapeDtypeStruct((count, width), BF),
            jax.ShapeDtypeStruct((count, width), BF),
            jax.ShapeDtypeStruct((count, top), F32),
            jax.ShapeDtypeStruct((1, depth, units), F32),
        ),
        in_specs=[vmem] * 6 + [hbm] * 3,
        out_specs=(vmem,) * 4,
        scratch_shapes=[
            pltpu.VMEM((3, n, depth, units), BF),
            rows, rows, rows, rows,
            pltpu.VMEM((slots, units), BF),
            pltpu.VMEM((slots, units), F32),
            pltpu.VMEM((slots, units), F32),
            pltpu.VMEM((slots, units), BF),
            pltpu.VMEM((slots, units), BF),
            shards, shards, shards, shards,
            pltpu.VMEM((width, units), F32),
            pltpu.VMEM((n, depth, units), BF),
            pltpu.VMEM((2, n, depth, units), BF),
            pltpu.VMEM((top, count, slots), BF),
            dma((3,)),
            dma((2, 3, n - 1)), dma((2, 3, n - 1)),
            dma((2, owners)), dma((2, owners)),
            dma((n, owners)), dma((n, owners)),
            dma((n, owners)), dma((n, owners)),
            dma((2, n)), dma((2, n)),
        ],
        compiler_params=pltpu.CompilerParams(
            collective_id=0, has_side_effects=True, vmem_limit_bytes=56 * 1024 * 1024
        ),
    )(first_out, second_out, first_grad, second_grad, routes, gate_values, w_gate, w_up, w_down)


def solution(mesh):
    rows = P(("dp", "expert"), None)
    mats = P("expert", "dp", None)
    return jax.shard_map(
        per_device,
        mesh=mesh,
        in_specs=(rows,) * 6 + (mats,) * 3,
        out_specs=(rows, rows, rows, mats),
        check_vma=False,
    )
```

```python
import functools
import math

import jax
import jax.numpy as jnp
from jax import lax
from jax.experimental import pallas as pl
from jax.experimental.pallas import tpu as pltpu
from jax.sharding import PartitionSpec as P

BF = jnp.bfloat16
F32 = jnp.float32
MESH = pl.DeviceIdType.MESH


def mm(a, b, ca, cb):
    return lax.dot_general(a, b, (((ca,), (cb,)), ((), ())), preferred_element_type=F32)


def tiles(extent, size=256):
    size = min(size, extent)
    return [slice(at, at + size) for at in range(0, extent, size)]


def layer_kernel(
    n, owners, cap, scale,
    x_ref, so_ref, fg_ref, sg_ref, routes_ref, gv_ref, wg_hbm, wu_hbm, wd_hbm,
    si_ref, ft_ref, gg_ref, wdg_ref,
    wbuf, s_in, s_cot, r_in, r_cot, hid, act, fac, gc, uc,
    o_out, b_out, o_cot, b_cot, part, rs_send, rs_recv, qbuf,
    lsem, wss, wrs, ass, ars, oss, ors, css, crs, rss, rrs,
):
    z = lax.axis_index("dp")
    me = lax.axis_index("expert")
    count, width = x_ref.shape
    top = routes_ref.shape[0]
    slots = owners * cap
    depth, units = wbuf.shape[2], wbuf.shape[3]

    def peers(body):
        def step(o, carry):
            body(o, lax.rem(me + o, owners))
            return carry
        lax.fori_loop(1, owners, step, 0)

    barrier = pltpu.get_barrier_semaphore()
    peers(lambda o, to: pl.semaphore_signal(
        barrier, inc=1, device_id={"expert": to}, device_id_type=MESH))
    for s in range(1, n):
        pl.semaphore_signal(
            barrier, inc=1, device_id={"dp": lax.rem(z + s, n)}, device_id_type=MESH)

    local = [
        pltpu.make_async_copy(w.at[0], wbuf.at[m, z], lsem.at[m])
        for m, w in enumerate((wg_hbm, wu_hbm, wd_hbm))
    ]
    for copy in local:
        copy.start()

    eye = (
        lax.broadcasted_iota(jnp.int32, (count, count), 0)
        == lax.broadcasted_iota(jnp.int32, (count, count), 1)
    )

    def column(row):
        return jnp.sum(jnp.where(eye, row, jnp.zeros_like(row)), axis=1, keepdims=True)

    def as_row(col):
        return jnp.sum(jnp.where(eye, col, jnp.zeros_like(col)), axis=0, keepdims=True)

    routes = [column(routes_ref[k:k + 1, :]) for k in range(top)]
    gates = [column(gv_ref[k:k + 1, :]) for k in range(top)]
    ids = lax.broadcasted_iota(jnp.int32, (count, owners), 1)
    lower = (
        lax.broadcasted_iota(jnp.int32, (count, count), 1)
        < lax.broadcasted_iota(jnp.int32, (count, count), 0)
    ).astype(F32).astype(BF)
    slot_ids = lax.broadcasted_iota(jnp.int32, (count, slots), 1)
    base = jnp.zeros((1, owners), F32)
    for k in range(top):
        onehot = (routes[k] == ids).astype(F32)
        before = mm(lower, onehot.astype(BF), 1, 0) + base
        place = jnp.sum(onehot * (before + ids.astype(F32) * cap), axis=1, keepdims=True)
        base = base + jnp.sum(onehot, axis=0, keepdims=True)
        qbuf[k] = (place.astype(jnp.int32) == slot_ids).astype(F32).astype(BF)

    def wcopy(m, s, way, shard, to):
        return pltpu.make_async_remote_copy(
            src_ref=wbuf.at[m, shard], dst_ref=wbuf.at[m, shard],
            send_sem=wss.at[way, m, s], recv_sem=wrs.at[way, m, s],
            device_id={"dp": to}, device_id_type=MESH)

    def wsend(m, s, finish=False):
        @pl.when((z >= s) & (z < n - 1))
        def _():
            copy = wcopy(m, s, 0, z - s, z + 1)
            copy.wait_send() if finish else copy.start()

        @pl.when((z + s <= n - 1) & (z > 0))
        def _():
            copy = wcopy(m, s, 1, z + s, z - 1)
            copy.wait_send() if finish else copy.start()

    def wrecv(m, s):
        @pl.when(z - 1 - s >= 0)
        def _():
            wcopy(m, s, 0, z - 1 - s, z - 1).wait_recv()

        @pl.when(z + 1 + s <= n - 1)
        def _():
            wcopy(m, s, 1, z + 1 + s, z + 1).wait_recv()

    def dsend(finish=False):
        for s in reversed(range(n - 1)):
            @pl.when(z + 1 + s <= n - 1)
            def _():
                copy = wcopy(2, s, 0, z, z + 1 + s)
                copy.wait_send() if finish else copy.start()

            @pl.when(z - 1 - s >= 0)
            def _():
                copy = wcopy(2, s, 1, z, z - 1 - s)
                copy.wait_send() if finish else copy.start()

    for copy in local:
        copy.wait()
    pl.semaphore_wait(barrier, owners + n - 2)

    wsend(0, 0)
    wsend(1, 0)

    def acopy(a, o, to):
        src, dst = ((s_in, r_in), (s_cot, r_cot))[a]
        return pltpu.make_async_remote_copy(
            src_ref=src.at[to], dst_ref=dst.at[me],
            send_sem=ass.at[a, o], recv_sem=ars.at[a, o],
            device_id={"expert": to}, device_id_type=MESH)

    both = sum(qbuf[k].astype(F32) for k in range(top)).astype(BF)
    for c in tiles(width):
        rows = mm(both, x_ref[:, c], 0, 0).astype(BF)
        s_in[:, :, c] = rows.reshape(owners, cap, rows.shape[1])
    peers(lambda o, to: acopy(0, o, to).start())
    r_in[me] = s_in[me]
    for c in tiles(width):
        grads = sg_ref[:, c].astype(F32)
        rows = sum(
            mm(qbuf[k], (gates[k] * grads).astype(BF), 0, 0) for k in range(top)
        ).astype(BF)
        s_cot[:, :, c] = rows.reshape(owners, cap, rows.shape[1])
    peers(lambda o, to: acopy(1, o, to).start())
    r_cot[me] = s_cot[me]

    for s in range(n - 1):
        for m in (0, 1):
            wrecv(m, s)
            if s + 1 < n - 1:
                wsend(m, s + 1)
        if s == max(n - 3, 0):
            dsend()
    peers(lambda o, to: acopy(0, o, to).wait_recv())
    peers(lambda o, to: acopy(1, o, to).wait_recv())

    rows_in = r_in[...].reshape(slots, width)
    for c in tiles(units):
        size = c.stop - c.start
        pre_gate = mm(rows_in, wbuf[0, :, :, c].reshape(width, size), 1, 0)
        pre_up = mm(rows_in, wbuf[1, :, :, c].reshape(width, size), 1, 0)
        squashed = jax.nn.sigmoid(pre_gate)
        activated = pre_gate * squashed
        hid[:, c] = (activated * pre_up).astype(BF)
        act[:, c] = activated
        fac[:, c] = pre_up * squashed * (1.0 + pre_gate * (1.0 - squashed))

    def ocopy(j, o, to):
        return pltpu.make_async_remote_copy(
            src_ref=o_out.at[j, to], dst_ref=b_out.at[j, me],
            send_sem=oss.at[j, o], recv_sem=ors.at[j, o],
            device_id={"expert": to}, device_id_type=MESH)

    def out_shard(j):
        rows = mm(hid[...], wbuf[2, j], 1, 1).astype(BF)
        o_out[j] = rows.reshape(owners, cap, depth)
        peers(lambda o, to: ocopy(j, o, to).start())
        b_out[j, me] = o_out[j, me]

    out_shard(z)

    for c in tiles(width):
        part[c, :] = mm(r_cot[:, :, c].reshape(slots, c.stop - c.start), hid[...], 0, 0)

    def rcopy(way, j, to):
        return pltpu.make_async_remote_copy(
            src_ref=rs_send.at[j], dst_ref=rs_recv.at[way, j],
            send_sem=rss.at[way, j], recv_sem=rrs.at[way, j],
            device_id={"dp": to}, device_id_type=MESH)

    def rfirst(way, j):
        ahead = z + 1 if way == 0 else z - 1

        @pl.when((z == 0) & (z < j) if way == 0 else (z == n - 1) & (z > j))
        def _():
            rs_send[j] = part[j * depth:(j + 1) * depth, :].astype(BF)
            rcopy(way, j, ahead).start()

    def rstep(way, j):
        behind = z - 1 if way == 0 else z + 1
        ahead = z + 1 if way == 0 else z - 1

        @pl.when((z > 0) & (z < j) if way == 0 else (z < n - 1) & (z > j))
        def _():
            rcopy(way, j, behind).wait_recv()
            mine = part[j * depth:(j + 1) * depth, :]
            rs_send[j] = (mine + rs_recv[way, j].astype(F32)).astype(BF)
            rcopy(way, j, ahead).start()

    for s in range(n - 1):
        rfirst(0, n - 1 - s)
        rfirst(1, s)

    for s in range(n - 1):
        wrecv(2, s)

        @pl.when(z - 1 - s >= 0)
        def _():
            out_shard(z - 1 - s)

        @pl.when(z + 1 + s <= n - 1)
        def _():
            out_shard(z + 1 + s)

        if s < n - 2:
            rstep(0, n - 1 - s)
            rstep(1, s)

    rows_cot = r_cot[...].reshape(slots, width)
    for c in tiles(units):
        hidden_cot = mm(rows_cot, wbuf[2, :, :, c].reshape(width, c.stop - c.start), 1, 0)
        gc[:, c] = (hidden_cot * fac[:, c]).astype(BF)
        uc[:, c] = (hidden_cot * act[:, c]).astype(BF)

    def ccopy(j, o, to):
        return pltpu.make_async_remote_copy(
            src_ref=o_cot.at[j, to], dst_ref=b_cot.at[j, me],
            send_sem=css.at[j, o], recv_sem=crs.at[j, o],
            device_id={"expert": to}, device_id_type=MESH)

    def cot_shard(j, carry):
        rows = mm(gc[...], wbuf[0, j], 1, 1) + mm(uc[...], wbuf[1, j], 1, 1)
        o_cot[j] = rows.astype(BF).reshape(owners, cap, depth)
        peers(lambda o, to: ccopy(j, o, to).start())
        b_cot[j, me] = o_cot[j, me]
        return carry

    lax.fori_loop(0, n, cot_shard, 0)

    sums = [jnp.zeros((count, 1), F32) for _ in range(top)]
    for j in range(n):
        c = slice(j * depth, (j + 1) * depth)
        peers(lambda o, to: ocopy(j, o, to).wait_recv())
        rows = b_out[j].reshape(slots, depth)
        combined = jnp.zeros((count, depth), F32)
        grads = sg_ref[:, c].astype(F32)
        for k in range(top):
            chosen = mm(qbuf[k], rows, 1, 0)
            combined = combined + gates[k] * chosen
            sums[k] = sums[k] + jnp.sum(grads * chosen, axis=1, keepdims=True)
        si_ref[:, c] = (so_ref[:, c].astype(F32) - combined).astype(BF)
    for k in range(top):
        gg_ref[k:k + 1, :] = as_row(sums[k])

    own = pl.ds(pl.multiple_of(z * depth, depth), depth)

    @pl.when(z > 0)
    def _():
        rcopy(0, z, z - 1).wait_recv()
        part[own, :] = part[own, :] + rs_recv[0, z].astype(F32)

    @pl.when(z < n - 1)
    def _():
        rcopy(1, z, z + 1).wait_recv()
        part[own, :] = part[own, :] + rs_recv[1, z].astype(F32)

    wdg_ref[0] = part[own, :] * scale

    both = sum(qbuf[k].astype(F32) for k in range(top)).astype(BF)
    for j in range(n):
        c = slice(j * depth, (j + 1) * depth)
        peers(lambda o, to: ccopy(j, o, to).wait_recv())
        total = mm(both, b_cot[j].reshape(slots, depth), 1, 0)
        ft_ref[:, c] = (fg_ref[:, c].astype(F32) + total).astype(BF)

    dsend(finish=True)
    for s in range(n - 1):
        for m in (0, 1):
            wsend(m, s, finish=True)

        @pl.when(z < n - 1 - s)
        def _():
            rcopy(0, n - 1 - s, z + 1).wait_send()

        @pl.when(z > s)
        def _():
            rcopy(1, s, z - 1).wait_send()

    for a in (0, 1):
        peers(lambda o, to: acopy(a, o, to).wait_send())

    def sent(j, carry):
        peers(lambda o, to: ocopy(j, o, to).wait_send())
        peers(lambda o, to: ccopy(j, o, to).wait_send())
        return carry

    lax.fori_loop(0, n, sent, 0)


def per_device(
    first_out, second_out, first_grad, second_grad, routes, gate_values, w_gate, w_up, w_down
):
    count, width = first_out.shape
    top = routes.shape[1]
    owners = lax.axis_size("expert")
    n = lax.axis_size("dp")
    cap = min(count, 2 * count * top // owners)
    slots = owners * cap
    depth, units = w_gate.shape[1:]
    vmem = pl.BlockSpec(memory_space=pltpu.VMEM)
    hbm = pl.BlockSpec(memory_space=pl.ANY)
    dma = pltpu.SemaphoreType.DMA
    rows = pltpu.VMEM((owners, cap, width), BF)
    shards = pltpu.VMEM((n, owners, cap, depth), BF)
    second_in, first_total, gate_grad, down_grad = pl.pallas_call(
        functools.partial(layer_kernel, n, owners, cap, 1.0 / math.sqrt(count * n)),
        out_shape=(
            jax.ShapeDtypeStruct((count, width), BF),
            jax.ShapeDtypeStruct((count, width), BF),
            jax.ShapeDtypeStruct((top, count), F32),
            jax.ShapeDtypeStruct((1, depth, units), F32),
        ),
        in_specs=[vmem] * 6 + [hbm] * 3,
        out_specs=(vmem,) * 4,
        scratch_shapes=[
            pltpu.VMEM((3, n, depth, units), BF),
            rows, rows, rows, rows,
            pltpu.VMEM((slots, units), BF),
            pltpu.VMEM((slots, units), F32),
            pltpu.VMEM((slots, units), F32),
            pltpu.VMEM((slots, units), BF),
            pltpu.VMEM((slots, units), BF),
            shards, shards, shards, shards,
            pltpu.VMEM((width, units), F32),
            pltpu.VMEM((n, depth, units), BF),
            pltpu.VMEM((2, n, depth, units), BF),
            pltpu.VMEM((top, count, slots), BF),
            dma((3,)),
            dma((2, 3, n - 1)), dma((2, 3, n - 1)),
            dma((2, owners)), dma((2, owners)),
            dma((n, owners)), dma((n, owners)),
            dma((n, owners)), dma((n, owners)),
            dma((2, n)), dma((2, n)),
        ],
        compiler_params=pltpu.CompilerParams(
            collective_id=0, has_side_effects=True, vmem_limit_bytes=56 * 1024 * 1024
        ),
    )(
        first_out, second_out, first_grad, second_grad, routes.T, gate_values.T,
        w_gate, w_up, w_down,
    )
    return (second_in, first_total, gate_grad.T, down_grad)


def solution(mesh):
    rows = P(("dp", "expert"), None)
    mats = P("expert", "dp", None)
    return jax.shard_map(
        per_device,
        mesh=mesh,
        in_specs=(rows,) * 6 + (mats,) * 3,
        out_specs=(rows, rows, rows, mats),
        check_vma=False,
    )
```

```python
import functools
import math

import jax
import jax.numpy as jnp
from jax import lax
from jax.experimental import pallas as pl
from jax.experimental.pallas import tpu as pltpu
from jax.sharding import PartitionSpec as P

BF = jnp.bfloat16
F32 = jnp.float32
MESH = pl.DeviceIdType.MESH


def mm(a, b, ca, cb):
    return lax.dot_general(a, b, (((ca,), (cb,)), ((), ())), preferred_element_type=F32)


def tiles(extent, size=256):
    size = min(size, extent)
    return [slice(at, at + size) for at in range(0, extent, size)]


def layer_kernel(
    n, owners, cap, scale,
    x_ref, so_ref, fg_ref, sg_ref, routes_ref, gv_ref, wg_hbm, wu_hbm, wd_hbm,
    si_ref, ft_ref, gg_ref, wdg_ref,
    wbuf, s_in, s_cot, r_in, r_cot, hid, act, fac, gc, uc,
    o_out, b_out, o_cot, b_cot, part, rs_send, rs_recv, qbuf,
    lsem, wss, wrs, ass, ars, oss, ors, css, crs, rss, rrs,
):
    z = lax.axis_index("dp")
    me = lax.axis_index("expert")
    count, width = x_ref.shape
    top = routes_ref.shape[0]
    slots = owners * cap
    depth, units = wbuf.shape[2], wbuf.shape[3]

    def peers(body):
        def step(o, carry):
            body(o, lax.rem(me + o, owners))
            return carry
        lax.fori_loop(1, owners, step, 0)

    barrier = pltpu.get_barrier_semaphore()
    peers(lambda o, to: pl.semaphore_signal(
        barrier, inc=1, device_id={"expert": to}, device_id_type=MESH))
    for s in range(1, n):
        pl.semaphore_signal(
            barrier, inc=1, device_id={"dp": lax.rem(z + s, n)}, device_id_type=MESH)

    local = [
        pltpu.make_async_copy(w.at[0], wbuf.at[m, z], lsem.at[m])
        for m, w in enumerate((wg_hbm, wu_hbm, wd_hbm))
    ]
    for copy in local:
        copy.start()

    eye = (
        lax.broadcasted_iota(jnp.int32, (count, count), 0)
        == lax.broadcasted_iota(jnp.int32, (count, count), 1)
    )

    def column(row):
        return jnp.sum(jnp.where(eye, row, jnp.zeros_like(row)), axis=1, keepdims=True)

    def as_row(col):
        return jnp.sum(jnp.where(eye, col, jnp.zeros_like(col)), axis=0, keepdims=True)

    routes = [column(routes_ref[k:k + 1, :]) for k in range(top)]
    gates = [column(gv_ref[k:k + 1, :]) for k in range(top)]
    ids = lax.broadcasted_iota(jnp.int32, (count, owners), 1)
    lower = (
        lax.broadcasted_iota(jnp.int32, (count, count), 1)
        < lax.broadcasted_iota(jnp.int32, (count, count), 0)
    ).astype(F32).astype(BF)
    slot_ids = lax.broadcasted_iota(jnp.int32, (count, slots), 1)
    base = jnp.zeros((1, owners), F32)
    for k in range(top):
        onehot = (routes[k] == ids).astype(F32)
        before = mm(lower, onehot.astype(BF), 1, 0) + base
        place = jnp.sum(onehot * (before + ids.astype(F32) * cap), axis=1, keepdims=True)
        base = base + jnp.sum(onehot, axis=0, keepdims=True)
        qbuf[k] = (place.astype(jnp.int32) == slot_ids).astype(F32).astype(BF)

    def wcopy(m, s, way, shard, to):
        return pltpu.make_async_remote_copy(
            src_ref=wbuf.at[m, shard], dst_ref=wbuf.at[m, shard],
            send_sem=wss.at[way, m, s], recv_sem=wrs.at[way, m, s],
            device_id={"dp": to}, device_id_type=MESH)

    def wsend(m, s, finish=False):
        @pl.when((z >= s) & (z < n - 1))
        def _():
            copy = wcopy(m, s, 0, z - s, z + 1)
            copy.wait_send() if finish else copy.start()

        @pl.when((z + s <= n - 1) & (z > 0))
        def _():
            copy = wcopy(m, s, 1, z + s, z - 1)
            copy.wait_send() if finish else copy.start()

    def wrecv(m, s):
        @pl.when(z - 1 - s >= 0)
        def _():
            wcopy(m, s, 0, z - 1 - s, z - 1).wait_recv()

        @pl.when(z + 1 + s <= n - 1)
        def _():
            wcopy(m, s, 1, z + 1 + s, z + 1).wait_recv()

    at_end = (z == 0) | (z == n - 1)
    between = (z > 0) & (z < n - 1)

    def dsend(s, where, finish=False):
        @pl.when(where & (z + 1 + s <= n - 1))
        def _():
            copy = wcopy(2, s, 0, z, z + 1 + s)
            copy.wait_send() if finish else copy.start()

        @pl.when(where & (z - 1 - s >= 0))
        def _():
            copy = wcopy(2, s, 1, z, z - 1 - s)
            copy.wait_send() if finish else copy.start()

    for copy in local:
        copy.wait()
    pl.semaphore_wait(barrier, owners + n - 2)

    wsend(0, 0)
    wsend(1, 0)

    def acopy(a, o, to):
        src, dst = ((s_in, r_in), (s_cot, r_cot))[a]
        return pltpu.make_async_remote_copy(
            src_ref=src.at[to], dst_ref=dst.at[me],
            send_sem=ass.at[a, o], recv_sem=ars.at[a, o],
            device_id={"expert": to}, device_id_type=MESH)

    both = sum(qbuf[k].astype(F32) for k in range(top)).astype(BF)
    for c in tiles(width):
        rows = mm(both, x_ref[:, c], 0, 0).astype(BF)
        s_in[:, :, c] = rows.reshape(owners, cap, rows.shape[1])
    peers(lambda o, to: acopy(0, o, to).start())
    r_in[me] = s_in[me]
    for c in tiles(width):
        grads = sg_ref[:, c].astype(F32)
        rows = sum(
            mm(qbuf[k], (gates[k] * grads).astype(BF), 0, 0) for k in range(top)
        ).astype(BF)
        s_cot[:, :, c] = rows.reshape(owners, cap, rows.shape[1])
    peers(lambda o, to: acopy(1, o, to).start())
    r_cot[me] = s_cot[me]

    for s in range(n - 1):
        for m in (0, 1):
            wrecv(m, s)
            if s + 1 < n - 1:
                wsend(m, s + 1)
        dsend(s, at_end)
    peers(lambda o, to: acopy(0, o, to).wait_recv())
    peers(lambda o, to: acopy(1, o, to).wait_recv())

    rows_in = r_in[...].reshape(slots, width)
    for c in tiles(units):
        size = c.stop - c.start
        pre_gate = mm(rows_in, wbuf[0, :, :, c].reshape(width, size), 1, 0)
        pre_up = mm(rows_in, wbuf[1, :, :, c].reshape(width, size), 1, 0)
        squashed = jax.nn.sigmoid(pre_gate)
        activated = pre_gate * squashed
        hid[:, c] = (activated * pre_up).astype(BF)
        act[:, c] = activated
        fac[:, c] = pre_up * squashed * (1.0 + pre_gate * (1.0 - squashed))

    for s in range(n - 1):
        for m in (0, 1):
            wsend(m, s, finish=True)
    for s in range(n - 1):
        dsend(s, between)

    def ocopy(j, o, to):
        return pltpu.make_async_remote_copy(
            src_ref=o_out.at[j, to], dst_ref=b_out.at[j, me],
            send_sem=oss.at[j, o], recv_sem=ors.at[j, o],
            device_id={"expert": to}, device_id_type=MESH)

    def out_shard(j):
        rows = mm(hid[...], wbuf[2, j], 1, 1).astype(BF)
        o_out[j] = rows.reshape(owners, cap, depth)
        peers(lambda o, to: ocopy(j, o, to).start())
        b_out[j, me] = o_out[j, me]

    out_shard(z)

    for c in tiles(width):
        part[c, :] = mm(r_cot[:, :, c].reshape(slots, c.stop - c.start), hid[...], 0, 0)

    def rcopy(way, j, to):
        return pltpu.make_async_remote_copy(
            src_ref=rs_send.at[j], dst_ref=rs_recv.at[way, j],
            send_sem=rss.at[way, j], recv_sem=rrs.at[way, j],
            device_id={"dp": to}, device_id_type=MESH)

    def rfirst(way, j):
        ahead = z + 1 if way == 0 else z - 1

        @pl.when((z == 0) & (z < j) if way == 0 else (z == n - 1) & (z > j))
        def _():
            rs_send[j] = part[j * depth:(j + 1) * depth, :].astype(BF)
            rcopy(way, j, ahead).start()

    def rstep(way, j):
        behind = z - 1 if way == 0 else z + 1
        ahead = z + 1 if way == 0 else z - 1

        @pl.when((z > 0) & (z < j) if way == 0 else (z < n - 1) & (z > j))
        def _():
            rcopy(way, j, behind).wait_recv()
            mine = part[j * depth:(j + 1) * depth, :]
            rs_send[j] = (mine + rs_recv[way, j].astype(F32)).astype(BF)
            rcopy(way, j, ahead).start()

    for s in range(n - 1):
        rfirst(0, n - 1 - s)
        rfirst(1, s)

    for s in range(n - 1):
        wrecv(2, s)

        @pl.when(z - 1 - s >= 0)
        def _():
            out_shard(z - 1 - s)

        @pl.when(z + 1 + s <= n - 1)
        def _():
            out_shard(z + 1 + s)

        if s < n - 2:
            rstep(0, n - 1 - s)
            rstep(1, s)

    rows_cot = r_cot[...].reshape(slots, width)
    for c in tiles(units):
        hidden_cot = mm(rows_cot, wbuf[2, :, :, c].reshape(width, c.stop - c.start), 1, 0)
        gc[:, c] = (hidden_cot * fac[:, c]).astype(BF)
        uc[:, c] = (hidden_cot * act[:, c]).astype(BF)

    def ccopy(j, o, to):
        return pltpu.make_async_remote_copy(
            src_ref=o_cot.at[j, to], dst_ref=b_cot.at[j, me],
            send_sem=css.at[j, o], recv_sem=crs.at[j, o],
            device_id={"expert": to}, device_id_type=MESH)

    def cot_shard(j, carry):
        rows = mm(gc[...], wbuf[0, j], 1, 1) + mm(uc[...], wbuf[1, j], 1, 1)
        o_cot[j] = rows.astype(BF).reshape(owners, cap, depth)
        peers(lambda o, to: ccopy(j, o, to).start())
        b_cot[j, me] = o_cot[j, me]
        return carry

    lax.fori_loop(0, n, cot_shard, 0)

    sums = [jnp.zeros((count, 1), F32) for _ in range(top)]
    for j in range(n):
        c = slice(j * depth, (j + 1) * depth)
        peers(lambda o, to: ocopy(j, o, to).wait_recv())
        rows = b_out[j].reshape(slots, depth)
        combined = jnp.zeros((count, depth), F32)
        grads = sg_ref[:, c].astype(F32)
        for k in range(top):
            chosen = mm(qbuf[k], rows, 1, 0)
            combined = combined + gates[k] * chosen
            sums[k] = sums[k] + jnp.sum(grads * chosen, axis=1, keepdims=True)
        si_ref[:, c] = (so_ref[:, c].astype(F32) - combined).astype(BF)
    for k in range(top):
        gg_ref[k:k + 1, :] = as_row(sums[k])

    own = pl.ds(pl.multiple_of(z * depth, depth), depth)

    @pl.when(z > 0)
    def _():
        rcopy(0, z, z - 1).wait_recv()
        part[own, :] = part[own, :] + rs_recv[0, z].astype(F32)

    @pl.when(z < n - 1)
    def _():
        rcopy(1, z, z + 1).wait_recv()
        part[own, :] = part[own, :] + rs_recv[1, z].astype(F32)

    wdg_ref[0] = part[own, :] * scale

    both = sum(qbuf[k].astype(F32) for k in range(top)).astype(BF)
    for j in range(n):
        c = slice(j * depth, (j + 1) * depth)
        peers(lambda o, to: ccopy(j, o, to).wait_recv())
        total = mm(both, b_cot[j].reshape(slots, depth), 1, 0)
        ft_ref[:, c] = (fg_ref[:, c].astype(F32) + total).astype(BF)

    for s in range(n - 1):
        dsend(s, at_end, finish=True)
        dsend(s, between, finish=True)

        @pl.when(z < n - 1 - s)
        def _():
            rcopy(0, n - 1 - s, z + 1).wait_send()

        @pl.when(z > s)
        def _():
            rcopy(1, s, z - 1).wait_send()

    for a in (0, 1):
        peers(lambda o, to: acopy(a, o, to).wait_send())

    def sent(j, carry):
        peers(lambda o, to: ocopy(j, o, to).wait_send())
        peers(lambda o, to: ccopy(j, o, to).wait_send())
        return carry

    lax.fori_loop(0, n, sent, 0)


def per_device(
    first_out, second_out, first_grad, second_grad, routes, gate_values, w_gate, w_up, w_down
):
    count, width = first_out.shape
    top = routes.shape[1]
    owners = lax.axis_size("expert")
    n = lax.axis_size("dp")
    cap = min(count, 2 * count * top // owners)
    slots = owners * cap
    depth, units = w_gate.shape[1:]
    vmem = pl.BlockSpec(memory_space=pltpu.VMEM)
    hbm = pl.BlockSpec(memory_space=pl.ANY)
    dma = pltpu.SemaphoreType.DMA
    rows = pltpu.VMEM((owners, cap, width), BF)
    shards = pltpu.VMEM((n, owners, cap, depth), BF)
    second_in, first_total, gate_grad, down_grad = pl.pallas_call(
        functools.partial(layer_kernel, n, owners, cap, 1.0 / math.sqrt(count * n)),
        out_shape=(
            jax.ShapeDtypeStruct((count, width), BF),
            jax.ShapeDtypeStruct((count, width), BF),
            jax.ShapeDtypeStruct((top, count), F32),
            jax.ShapeDtypeStruct((1, depth, units), F32),
        ),
        in_specs=[vmem] * 6 + [hbm] * 3,
        out_specs=(vmem,) * 4,
        scratch_shapes=[
            pltpu.VMEM((3, n, depth, units), BF),
            rows, rows, rows, rows,
            pltpu.VMEM((slots, units), BF),
            pltpu.VMEM((slots, units), F32),
            pltpu.VMEM((slots, units), F32),
            pltpu.VMEM((slots, units), BF),
            pltpu.VMEM((slots, units), BF),
            shards, shards, shards, shards,
            pltpu.VMEM((width, units), F32),
            pltpu.VMEM((n, depth, units), BF),
            pltpu.VMEM((2, n, depth, units), BF),
            pltpu.VMEM((top, count, slots), BF),
            dma((3,)),
            dma((2, 3, n - 1)), dma((2, 3, n - 1)),
            dma((2, owners)), dma((2, owners)),
            dma((n, owners)), dma((n, owners)),
            dma((n, owners)), dma((n, owners)),
            dma((2, n)), dma((2, n)),
        ],
        compiler_params=pltpu.CompilerParams(
            collective_id=0, has_side_effects=True, vmem_limit_bytes=56 * 1024 * 1024
        ),
    )(
        first_out, second_out, first_grad, second_grad, routes.T, gate_values.T,
        w_gate, w_up, w_down,
    )
    return (second_in, first_total, gate_grad.T, down_grad)


def solution(mesh):
    rows = P(("dp", "expert"), None)
    mats = P("expert", "dp", None)
    return jax.shard_map(
        per_device,
        mesh=mesh,
        in_specs=(rows,) * 6 + (mats,) * 3,
        out_specs=(rows, rows, rows, mats),
        check_vma=False,
    )
```
